1024 devices in a mesh: dp: 64 (over y, z_lo, core), col: 16 (over x, z_hi).
Axes of the slice: x: 4, y: 4, z: 32 (z_hi: 4, z_lo: 8; z = z_hi * 8 + z_lo), core: 2. Of those that a mesh axis runs over, the one named last changes fastest.
Arguments:
- embedded: bfloat16 [32768, 2048], P('dp', 'col'), may hold values from -6 to 6
- gate: bfloat16 [32768, 2048], P('dp', 'col'), may hold values from -6 to 6
- pre_hidden: bfloat16 [32768, 4096], P('dp', 'col'), may hold values from -6 to 6
- hidden_weight: bfloat16 [2048, 4096], P(None, 'col'), may hold values from -0.125 to 0.125
- cross_weight: bfloat16 [2048, 2048], P('col'), may hold values from -0.125 to 0.125
- out_weight: bfloat16 [4096], P('col'), may hold values from -5 to 5
- upstream: float32 [32768], P('dp'), may hold values from -6 to 6
- hot_rows: int32 [262144, 2], P('dp'), may hold values from 0 to 511
- cold_owner: int32 [262144, 2], P('dp'), may hold values from 0 to 63, as said below
- cold_rows: int32 [262144, 2], P('dp'), may hold values from 0 to 511
- hot_flag: int32 [262144, 2], P('dp'), may hold values from 0 to 1
- bag_sizes: int32 [262144], P('dp'), may hold values from 1 to 2
Outputs:
- hot_grad: float32 [256, 512], P('col', 'dp')
- cold_grad: float32 [256, 32768], P('col', 'dp')
The draws below stay inside these ranges and needn't reach their ends.
Inputs may be any that keep to these rules, and one draw needn't show every extreme that they name: `cold_owner`: the slots of a bag name different owners; among the slots of one device's 512 samples no owner is named more than 160 times; one owner, the same for every device, is named exactly 160 times by each device's slots, and every slot that names it is live (its bag holds 2 ids) and has hot_flag 0.
All inputs are finite; a program needn't handle non-finite values.
Results may differ from the reference program's by a relative error of at most 0.025.
Values may be sent and summed in bfloat16 or wider, within the bound.
No kernel may reach another device: no remote copies, remote signals or barrier semaphores. Data moves between devices by JAX's collectives and lax.ppermute only.
A program may use at most 128 MiB of HBM per device.

```python
import math
import jax
import jax.numpy as jnp
import numpy as np
from jax import lax

E = 256
H = 4096
F = 8
K = 2
B_DEV = 512
HOT = 512
COLD_DEV = 512
X = 2048
SAMPLES = 32768
COLD = 32768
CAP = 160
N_DP = 64
N_COL = 16


def routing_plan(key):
    bag_count = B_DEV * F
    heavy_key, order_key, side_key, label_key = jax.random.split(key, 4)
    heaviest = jax.random.randint(heavy_key, (), 0, N_DP, dtype=jnp.int32)
    orders = jax.vmap(lambda subkey: jax.random.permutation(subkey, bag_count))(jax.random.split(order_key, N_DP))
    placed = jnp.argsort(orders, axis=1).astype(jnp.int32)[:, :, None]
    heavy_side = jax.random.randint(side_key, (N_DP, bag_count, 1), 0, K, dtype=jnp.int32)
    slot_ids = jnp.arange(K, dtype=jnp.int32)[None, None, :]
    crowded = placed < CAP
    heavy_slot = crowded & (slot_ids == heavy_side)
    ranking = jnp.where(crowded, placed * (K - 1) + slot_ids - (slot_ids > heavy_side).astype(jnp.int32), CAP * (K - 1) + K * (placed - CAP) + slot_ids)
    labels = jax.vmap(lambda subkey: jax.random.permutation(subkey, N_DP - 1))(jax.random.split(label_key, N_DP)).astype(jnp.int32)
    picked = jnp.take_along_axis(labels, (ranking % (N_DP - 1)).reshape(N_DP, bag_count * K), axis=1).reshape(N_DP, bag_count, K)
    owners = jnp.where(heavy_slot, heaviest, (heaviest + 1 + picked) % N_DP)
    return (owners.reshape(N_DP * bag_count, K).astype(jnp.int32), heavy_slot.reshape(N_DP * bag_count, K), crowded.reshape(N_DP * bag_count))


def draw_cold_owner(key, part):
    owners, heavy_slot, crowded = routing_plan(key)
    return owners


def draw_hot_flag(key, part):
    owners, heavy_slot, crowded = routing_plan(key)
    key = jax.random.fold_in(key, 11)
    hot_mask = (jax.random.randint(key, owners.shape, 0, 4, dtype=jnp.int32) == 0).astype(jnp.int32)
    return jnp.where(heavy_slot, 0, hot_mask).astype(jnp.int32)


def draw_bag_sizes(key, part):
    owners, heavy_slot, crowded = routing_plan(key)
    key = jax.random.fold_in(key, 23)
    bag_draw = jax.random.randint(key, crowded.shape, 1, K + 1, dtype=jnp.int32)
    return jnp.where(crowded, K, bag_draw).astype(jnp.int32)


def touch_ends(drawn, rng, least, high):
    index_at = [jax.random.randint(jax.random.fold_in(rng, axis), (), 0, length) for axis, length in enumerate(drawn.shape)]
    main_axis = drawn.shape.index(max(drawn.shape))
    next_to = index_at[:main_axis] + [(index_at[main_axis] + 1) % drawn.shape[main_axis]] + index_at[main_axis + 1:]
    return drawn.at[tuple(index_at)].set(least).at[tuple(next_to)].set(high)


def levels(rng, extent, cuts, smallest, high):
    level = 1.0
    for axis_at, shards_of in cuts:
        draws = jax.random.uniform(jax.random.fold_in(jax.random.fold_in(rng, 6), axis_at), (shards_of,), jnp.float32, smallest / len(cuts), high / len(cuts))
        level = level * jnp.repeat(jnp.exp(draws), extent[axis_at] // shards_of).reshape((-1,) + (1,) * (len(extent) - 1 - axis_at))
    return level


def cumulative_ranks(count, skew):
    portions = [(1 << 20) // math.isqrt(rank ** skew) + 1 for rank in range(1, count + 1)]
    width = 1 + sum(portions) // (1 << 30)
    return np.cumsum(np.array([max(1, weight // width) for weight in portions]))


def ranked(rng, extent, amount, skew):
    listing = cumulative_ranks(amount, skew)
    pick = jax.random.randint(jax.random.fold_in(rng, 1), extent, 0, int(listing[amount - 1]))
    rank = jnp.searchsorted(jnp.asarray(listing, jnp.int32), pick, side="right")
    return jax.random.permutation(jax.random.fold_in(rng, 2), amount)[rank].astype(jnp.int32)


def normal_values(own_key, shape, scale, limit, pieces=(), kind=jnp.bfloat16):
    level = levels(own_key, shape, pieces, -0.22, 0.18) if pieces else 1.0
    values = jax.random.normal(own_key, shape, jnp.float32) * scale * level
    return jnp.minimum(jnp.maximum(values, -limit), limit).astype(kind)


def setup_inputs(seed: int = 0) -> dict:
    seeds = jax.random.split(jax.random.key(seed), 13)
    return {
        "embedded": normal_values(seeds[0], (SAMPLES, X), 1.0, 6.0, ((0, 64), (1, 16))),
        "gate": normal_values(seeds[1], (SAMPLES, X), 1.0, 6.0, ((0, 64), (1, 16))),
        "pre_hidden": normal_values(seeds[2], (SAMPLES, H), 1.0, 6.0, ((0, 64), (1, 16))),
        "hidden_weight": normal_values(seeds[3], (X, H), X ** -0.5, 0.125, ((1, 16),)),
        "cross_weight": normal_values(seeds[4], (X, X), X ** -0.5, 0.125, ((0, 16),)),
        "out_weight": normal_values(seeds[5], (H,), 1.0, 5.0, ((0, 16),)),
        "upstream": normal_values(seeds[6], (SAMPLES,), 1.0, 6.0, ((0, 64),), jnp.float32),
        "hot_rows": touch_ends(ranked(seeds[7], (SAMPLES * F, K), HOT, 1), jax.random.fold_in(seeds[7], 3), 0, HOT - 1).astype(jnp.int32),
        "cold_owner": draw_cold_owner(jax.random.fold_in(seeds[12], 71), 0),
        "cold_rows": touch_ends(jax.random.randint(seeds[9], (SAMPLES * F, K), 0, COLD_DEV), jax.random.fold_in(seeds[9], 1), 0, COLD_DEV - 1).astype(jnp.int32),
        "hot_flag": draw_hot_flag(jax.random.fold_in(seeds[12], 71), 0),
        "bag_sizes": draw_bag_sizes(jax.random.fold_in(seeds[12], 71), 0),
    }


def reference(embedded, gate, pre_hidden, hidden_weight, cross_weight, out_weight, upstream, hot_rows, cold_owner, cold_rows, hot_flag, bag_sizes):
    samples = embedded.shape[0]
    slope_rows = jnp.where(pre_hidden > 0, upstream[:, None] * out_weight.astype(jnp.float32)[None, :], 0.0).astype(jnp.bfloat16)
    hidden_cols = H // N_COL
    feature_cols = X // N_COL
    back_one = jnp.zeros((samples, X), jnp.float32)
    for group in range(N_COL):
        partial_value = jnp.dot(slope_rows[:, group * hidden_cols:(group + 1) * hidden_cols], hidden_weight[:, group * hidden_cols:(group + 1) * hidden_cols].T, preferred_element_type=jnp.float32)
        back_one = back_one + lax.optimization_barrier(partial_value.astype(jnp.bfloat16)).astype(jnp.float32)
    gated_prod = (back_one * embedded.astype(jnp.float32)).astype(jnp.bfloat16)
    crossed = jnp.zeros((samples, X), jnp.float32)
    for group in range(N_COL):
        partial_value = jnp.dot(gated_prod[:, group * feature_cols:(group + 1) * feature_cols], cross_weight[group * feature_cols:(group + 1) * feature_cols, :], preferred_element_type=jnp.float32)
        crossed = crossed + lax.optimization_barrier(partial_value.astype(jnp.bfloat16)).astype(jnp.float32)
    grad_embed = (back_one * (gate.astype(jnp.float32) + 1.0) + crossed).astype(jnp.bfloat16)
    vectors = grad_embed.reshape(samples, E, F).transpose(0, 2, 1).reshape(samples * F, 1, E)
    values = jnp.broadcast_to(vectors, (samples * F, K, E)).reshape(samples * F * K, E).astype(jnp.float32)
    slot_index = jnp.arange(K, dtype=jnp.int32)[None, :]
    active = slot_index < bag_sizes[:, None]
    is_hot = active & (hot_flag == 1)
    is_cold = active & (hot_flag == 0)
    hot_index = jnp.where(is_hot, hot_rows, HOT).reshape(-1)
    hot_grad = jax.ops.segment_sum(values, hot_index, HOT + 1)[:HOT].T
    cold_index = jnp.where(is_cold, cold_owner * COLD_DEV + cold_rows, COLD).reshape(-1)
    cold_grad = jax.ops.segment_sum(values, cold_index, COLD + 1)[:COLD].T
    return hot_grad, cold_grad
```

```python
import jax
import jax.numpy as jnp
from jax import lax
from jax.experimental import pallas as pl
from jax.experimental.pallas import tpu as pltpu
from jax.sharding import PartitionSpec as P

F = 8
HOT = 512
COLD_DEV = 512
CAP = 160
SIDE = 4
MAIN = 128
TAIL = CAP - MAIN
LANES = 256
MSG_ROWS = 24
F32 = jnp.float32
BF16 = jnp.bfloat16
PIECES = ("far_lo", "far_hi", "up_lo", "up_hi", "down_lo", "down_hi", "own")

NT = (((1,), (1,)), ((), ()))
TN = (((0,), (0,)), ((), ()))
NN = (((1,), (0,)), ((), ()))


def mxu(a, b, dims):
    return lax.dot_general(a, b, dims, preferred_element_type=F32)


def iota(shape, axis):
    return lax.broadcasted_iota(jnp.int32, shape, axis)


def one_hot(match):
    return jnp.where(match, 1.0, 0.0).astype(BF16)


def call(kernel, out_shape, inputs, smem=(), scratch=(), flops=0, moved=0):
    vmem = pl.BlockSpec(memory_space=pltpu.VMEM)
    scalar = pl.BlockSpec(memory_space=pltpu.SMEM)
    return pl.pallas_call(
        kernel,
        out_shape=out_shape,
        in_specs=[scalar] * len(smem) + [vmem] * len(inputs),
        out_specs=jax.tree.map(lambda _: vmem, out_shape),
        scratch_shapes=list(scratch),
        compiler_params=pltpu.CompilerParams(vmem_limit_bytes=40 * 2**20),
        cost_estimate=pl.CostEstimate(flops=flops, bytes_accessed=moved, transcendentals=0),
    )(*smem, *inputs)


def piece_shapes(rows, lanes):
    half = jax.ShapeDtypeStruct((rows // 2, lanes), BF16)
    return [half] * 6 + [jax.ShapeDtypeStruct((rows, lanes), BF16)]


def store_pieces(make, here, refs):
    half = refs[0].shape[0]
    for step, lo, hi in ((2, 0, 1), (1, 2, 3), (3, 4, 5)):
        block = make(lax.rem(here + step, SIDE))
        refs[lo][...] = block[:half].astype(BF16)
        refs[hi][...] = block[half:].astype(BF16)
    refs[6][...] = make(here).astype(BF16)


def hidden_kernel(here, weight, pre_hidden, upstream, out_weight, *refs):
    slope = jnp.where(
        pre_hidden[...] > 0, upstream[...] * out_weight[...].astype(F32), 0.0
    ).astype(BF16)
    rows = refs[6].shape[0]

    def make(block):
        start = pl.multiple_of(block * rows, rows)
        return mxu(weight[pl.ds(start, rows), :], slope, NT)

    store_pieces(make, here[0], refs)


def joined(own, below_lo, below_hi, above_lo, above_hi):
    half = own.shape[0] // 2
    lo = own[:half].astype(F32) + below_lo[...].astype(F32) + above_lo[...].astype(F32)
    hi = own[half:].astype(F32) + below_hi[...].astype(F32) + above_hi[...].astype(F32)
    return lo, hi


def mid_kernel(here, own, below_lo, below_hi, above_lo, above_hi, *refs):
    total = refs[7]
    lo, hi = joined(own, below_lo, below_hi, above_lo, above_hi)
    half = lo.shape[0]
    total[:half, :] = lo.astype(BF16)
    total[half:, :] = hi.astype(BF16)
    rows = refs[6].shape[0]

    def make(block):
        return total[pl.ds(pl.multiple_of(block * rows, rows), rows), :]

    store_pieces(make, here[0], refs[:7])


def cross_kernel(
    here, own, below_lo, below_hi, above_lo, above_hi, embedded, weight, back_one, *refs
):
    lo, hi = joined(own, below_lo, below_hi, above_lo, above_hi)
    total = jnp.concatenate([lo, hi], axis=0)
    back_one[...] = total
    gated = (total * embedded[...].astype(F32).T).astype(BF16)
    rows = refs[6].shape[0]

    def make(block):
        start = pl.multiple_of(block * rows, rows)
        return mxu(weight[:, pl.ds(start, rows)], gated, TN)

    store_pieces(make, here[0], refs)


def plan_kernel(owner, rows, flag, bags, source, target, part_a, part_b, part_c):
    width = 512
    owners = source.shape[0]
    ahead = one_hot(iota((width, width), 0) < iota((width, width), 1))
    owner_ids = iota((owners, width), 0)
    lane_slot = iota((LANES, width), 0)
    slot_ids = jnp.where(lane_slot < MAIN, lane_slot, MAIN + lane_slot % TAIL).astype(F32)
    for part in (part_a, part_b, part_c):
        part[...] = jnp.zeros_like(part)

    def step(chunk, used):
        at = pl.ds(pl.multiple_of(chunk * width, width), width)
        bag = chunk * width + iota((1, width), 1)
        for k in range(owner.shape[0]):
            cold = (bags[:, at] > k) & (flag[k : k + 1, at] == 0)
            hit = (owner_ids == owner[k : k + 1, at]) & cold
            match = one_hot(hit)
            before = mxu(match, ahead, NN) + used
            place = jnp.sum(jnp.where(hit, before, 0.0), axis=0, keepdims=True)
            taken = slot_ids == place
            row = rows[k : k + 1, at]
            for part, value in (
                (part_a, (bag >> 6) + 1),
                (part_b, (bag & 63) * 2 + (row & 1)),
                (part_c, row >> 1),
            ):
                part[...] += mxu(match, jnp.where(taken, value.astype(F32), 0.0).astype(BF16), NT)
            used = used + jnp.sum(jnp.where(hit, 1.0, 0.0), axis=1, keepdims=True)
        return used

    lax.fori_loop(0, owner.shape[1] // width, step, jnp.zeros((owners, 1), F32))
    high = part_a[...].astype(jnp.int32)
    low = part_b[...].astype(jnp.int32)
    top = part_c[...].astype(jnp.int32)
    source[...] = jnp.where(high > 0, (high - 1) * 64 + (low >> 1), -1)
    target[...] = jnp.where(high > 0, top * 2 + (low & 1), COLD_DEV)


def send_kernel(
    own, below_lo, below_hi, above_lo, above_hi, back_one, gate, source, hot_index, out, hot_rows
):
    lo, hi = joined(own, below_lo, below_hi, above_lo, above_hi)
    crossed = jnp.concatenate([lo, hi], axis=0)
    grad = (back_one[...] * (gate[...].astype(F32).T + 1.0) + crossed).astype(BF16)
    cols, samples = grad.shape
    wide = cols // F
    row_id = iota((cols, cols), 0)
    grad = mxu(
        one_hot(iota((cols, cols), 1) == (row_id % wide) * F + row_id // wide), grad, NN
    ).astype(BF16)

    owners = source.shape[0]
    share = HOT // owners
    hot_ids = iota((HOT, samples), 0)
    summed = jnp.zeros((HOT, cols), F32)
    for f in range(F):
        count = jnp.where(hot_ids == hot_index[f : f + 1, :], 1.0, 0.0)
        for k in range(1, hot_index.shape[0] // F):
            count += jnp.where(hot_ids == hot_index[k * F + f : k * F + f + 1, :], 1.0, 0.0)
        copies = jnp.concatenate([grad[f * wide : (f + 1) * wide]] * share, axis=0)
        summed += mxu(count.astype(BF16), copies, NT)
    keep = iota((HOT, cols), 1) // wide == iota((HOT, cols), 0) % share
    hot_rows[...] = jnp.sum(
        jnp.where(keep, summed, 0.0).reshape(owners, share, cols), axis=1
    )

    sample_ids = iota((samples, LANES), 0)
    tail_row = iota((wide, MAIN), 0)
    tail_keep = tail_row // 4 == iota((wide, MAIN), 1) // TAIL
    last_row = iota((8, MAIN), 0)

    def step(o, carry):
        pick = source[pl.ds(o, 1), :]
        found = mxu(grad, one_hot(sample_ids == (pick >> 3)), NN)
        feature = pick & 7
        value = jnp.where(feature == 0, found[:wide], 0.0)
        for f in range(1, F):
            value += jnp.where(feature == f, found[f * wide : (f + 1) * wide], 0.0)
        tail = jnp.where(tail_keep, value[:, MAIN:], 0.0)
        tail = tail[:8] + tail[8:]
        tail = tail + pltpu.roll(tail, 4, 0)
        hot = hot_rows[pl.ds(o, 1), :]
        hot_hi = hot.astype(BF16).astype(F32)
        last = jnp.where(
            last_row < 4,
            tail,
            jnp.where(last_row == 4, hot_hi, jnp.where(last_row == 5, hot - hot_hi, 0.0)),
        )
        out[o] = jnp.concatenate([value[:, :MAIN], last], axis=0).astype(BF16)
        return carry

    lax.fori_loop(0, owners, step, 0, unroll=4)


def gather_kernel(got, target, cold, hot):
    owners = got.shape[0]
    rows = cold.shape[1]
    wide = cold.shape[0]
    row_ids = iota((rows, LANES), 0)
    tail_keep = iota((wide, MAIN), 0) // 4 == iota((wide, MAIN), 1) // TAIL
    low_half = iota((8, MAIN), 0) < 4

    def step(o, carry):
        total, tails = carry
        block = got[o].astype(F32)
        last = block[wide:]
        tail = jnp.where(low_half, last, pltpu.roll(last, 4, 0))
        tail = jnp.where(tail_keep, jnp.concatenate([tail, tail], axis=0), 0.0)
        values = jnp.concatenate([block[:wide], tail], axis=1).astype(BF16)
        total = total + mxu(one_hot(row_ids == target[pl.ds(o, 1), :]), values, NT)
        return total, tails + last

    total, tails = lax.fori_loop(
        0,
        owners,
        step,
        (jnp.zeros((rows, wide), F32), jnp.zeros((8, MAIN), F32)),
        unroll=4,
    )
    cold[...] = total.T
    hot[...] = tails[4:5] + tails[5:6]


def ring_sum(pieces, axis_pairs):
    up, down = axis_pairs
    far_lo, far_hi, up_lo, up_hi, down_lo, down_hi, own = pieces

    def shift(x, pairs):
        return lax.ppermute(x, "col", pairs)

    def add(a, b):
        return (a.astype(F32) + b.astype(F32)).astype(BF16)

    first_up = shift(far_lo, up)
    first_down = shift(far_hi, down)
    below_hi = shift(up_hi, up)
    above_lo = shift(down_lo, down)
    below_lo = shift(add(first_up, up_lo), up)
    above_hi = shift(add(first_down, down_hi), down)
    return own, below_lo, below_hi, above_lo, above_hi


def local(
    embedded,
    gate,
    pre_hidden,
    hidden_weight,
    cross_weight,
    out_weight,
    upstream,
    hot_rows,
    cold_owner,
    cold_rows,
    hot_flag,
    bag_sizes,
):
    owners = lax.axis_size("dp")
    groups = lax.axis_size("col")
    samples, cols = embedded.shape
    inner = groups // SIDE
    total_cols = cross_weight.shape[1]
    wide = cols // F
    slots = hot_rows.shape[1]

    def ring(step_outer, step_inner):
        pairs = []
        for g in range(groups):
            outer, rest = divmod(g, inner)
            pairs.append(
                (g, (outer + step_outer) % SIDE * inner + (rest + step_inner) % inner)
            )
        return pairs

    outer_pairs = ring(1, 0), ring(-1, 0)
    inner_pairs = ring(0, 1), ring(0, -1)
    group = lax.axis_index("col")
    outer_here = (group // inner).reshape(1).astype(jnp.int32)
    inner_here = (group % inner).reshape(1).astype(jnp.int32)

    outer_rows = total_cols // SIDE
    pieces = call(
        hidden_kernel,
        piece_shapes(outer_rows, samples),
        (hidden_weight, pre_hidden, upstream[:, None], out_weight[None, :]),
        smem=(outer_here,),
        flops=2 * total_cols * samples * pre_hidden.shape[1],
        moved=4 * total_cols * samples,
    )

    source, target = call(
        plan_kernel,
        [jax.ShapeDtypeStruct((owners, LANES), jnp.int32)] * 2,
        (cold_owner.T, cold_rows.T, hot_flag.T, bag_sizes[None, :]),
        scratch=[pltpu.VMEM((owners, LANES), F32)] * 3,
        flops=2 * 10**9,
        moved=10**7,
    )
    got_rows = lax.all_to_all(
        target[:, :CAP].reshape(owners, 1, CAP), "dp", split_axis=0, concat_axis=0, tiled=True
    ).reshape(owners, CAP)
    got_rows = jnp.concatenate([got_rows[:, :MAIN]] + [got_rows[:, MAIN:]] * (MAIN // TAIL), axis=1)
    live = lax.broadcasted_iota(jnp.int32, hot_rows.shape, 1) < bag_sizes[:, None]
    hot_index = (
        jnp.where(live & (hot_flag == 1), hot_rows, -1)
        .T.reshape(slots, samples, F)
        .transpose(0, 2, 1)
        .reshape(slots * F, samples)
    )

    def stage_two(pieces):
        return call(
            mid_kernel,
            piece_shapes(cols, samples),
            ring_sum(pieces, outer_pairs),
            smem=(inner_here,),
            scratch=[pltpu.VMEM((outer_rows, samples), BF16)],
            flops=4 * outer_rows * samples,
            moved=10 * outer_rows * samples,
        )

    back = ring_sum(stage_two(pieces), inner_pairs)
    back_one, *pieces = call(
        cross_kernel,
        [jax.ShapeDtypeStruct((cols, samples), F32)] + piece_shapes(outer_rows, samples),
        back + (embedded, cross_weight),
        smem=(outer_here,),
        flops=2 * total_cols * samples * cols,
        moved=4 * total_cols * samples,
    )
    crossed = ring_sum(stage_two(pieces), inner_pairs)
    message = call(
        send_kernel,
        jax.ShapeDtypeStruct((owners, MSG_ROWS, MAIN), BF16),
        crossed + (back_one, gate, source, hot_index),
        scratch=[pltpu.VMEM((owners, cols), F32)],
        flops=2 * 10**9,
        moved=10**7,
    )
    got = lax.all_to_all(message, "dp", split_axis=0, concat_axis=0, tiled=True)
    cold_grad, hot_sum = call(
        gather_kernel,
        [
            jax.ShapeDtypeStruct((wide, COLD_DEV), F32),
            jax.ShapeDtypeStruct((1, MAIN), F32),
        ],
        (got, got_rows),
        flops=2 * 10**9,
        moved=10**7,
    )
    hot_grad = hot_sum.reshape(HOT // owners, wide).T
    return (hot_grad, cold_grad)


def solution(mesh):
    in_specs = (
        P("dp", "col"),
        P("dp", "col"),
        P("dp", "col"),
        P(None, "col"),
        P("col", None),
        P("col"),
        P("dp"),
        P("dp", None),
        P("dp", None),
        P("dp", None),
        P("dp", None),
        P("dp"),
    )
    out_specs = (P("col", "dp"), P("col", "dp"))
    return jax.shard_map(local, mesh=mesh, in_specs=in_specs, out_specs=out_specs, check_vma=False)
```

```python
import jax
import jax.numpy as jnp
from jax import lax
from jax.experimental import pallas as pl
from jax.experimental.pallas import tpu as pltpu
from jax.sharding import PartitionSpec as P

F = 8
HOT = 512
COLD_DEV = 512
CAP = 160
SIDE = 4
MAIN = 128
TAIL = CAP - MAIN
LANES = 256
HALF = 256
MSG_ROWS = 24
F32 = jnp.float32
BF16 = jnp.bfloat16
NT = (((1,), (1,)), ((), ()))
TN = (((0,), (0,)), ((), ()))
NN = (((1,), (0,)), ((), ()))


def mxu(a, b, dims):
    return lax.dot_general(a, b, dims, preferred_element_type=F32)


def iota(shape, axis):
    return lax.broadcasted_iota(jnp.int32, shape, axis)


def one_hot(match):
    return jnp.where(match, 1.0, 0.0).astype(BF16)


def call(kernel, out_shape, inputs, smem=(), scratch=(), flops=0, moved=0):
    vmem = pl.BlockSpec(memory_space=pltpu.VMEM)
    scalar = pl.BlockSpec(memory_space=pltpu.SMEM)
    return pl.pallas_call(
        kernel,
        out_shape=out_shape,
        in_specs=[scalar] * len(smem) + [vmem] * len(inputs),
        out_specs=jax.tree.map(lambda _: vmem, out_shape),
        scratch_shapes=list(scratch),
        compiler_params=pltpu.CompilerParams(vmem_limit_bytes=40 * 2**20),
        cost_estimate=pl.CostEstimate(flops=flops, bytes_accessed=moved, transcendentals=0),
    )(*smem, *inputs)


def blocks_of(rows, lanes):
    return [jax.ShapeDtypeStruct((rows, lanes), BF16)] * 4


def partner(here, flip):
    return jnp.where(flip == 0, here ^ 1, SIDE - 1 - here)


def store_blocks(make, place, diagonal, near, second, own):
    here, side = place[0], place[1]
    for ref, block in (
        (diagonal, (here + 2) % SIDE),
        (near, partner(here, side)),
        (second, partner(here, 1 - side)),
        (own, here),
    ):
        ref[...] = make(block).astype(BF16)


def hidden_kernel(place, weight, pre_hidden, upstream, out_weight, *refs):
    slope = jnp.where(
        pre_hidden[...] > 0, upstream[...] * out_weight[...].astype(F32), 0.0
    ).astype(BF16)
    rows = refs[0].shape[0]

    def make(block):
        start = pl.multiple_of(block * rows, rows)
        return mxu(weight[pl.ds(start, rows), :], slope, NT)

    store_blocks(make, place, *refs)


def joined(terms):
    own, near, far = terms
    return own[...].astype(F32) + near[...].astype(F32) + far[...].astype(F32)


def mid_kernel(place, own, near, far, *refs):
    total = refs[4]
    total[...] = joined((own, near, far)).astype(BF16)
    rows = refs[0].shape[0]

    def make(block):
        return total[pl.ds(pl.multiple_of(block * rows, rows), rows), :]

    store_blocks(make, place, *refs[:4])


def cross_kernel(place, own, near, far, embedded, weight, back_one, *refs):
    total = joined((own, near, far))
    back_one[...] = total
    gated = (total * embedded[...].astype(F32).T).astype(BF16)
    rows = refs[0].shape[0]

    def make(block):
        start = pl.multiple_of(block * rows, rows)
        return mxu(weight[:, pl.ds(start, rows)], gated, TN)

    store_blocks(make, place, *refs)


def row_code(row):
    return ((MAIN + (row & (MAIN - 1))) << (row >> 7)).astype(F32)


def plan_kernel(owner, rows, flag, bags, group, sample, code):
    width = 512
    owners = group.shape[0]
    ahead = one_hot(iota((width, width), 0) < iota((width, width), 1))
    owner_ids = iota((owners, width), 0)
    lane_slot = iota((LANES, width), 0)
    slot_ids = jnp.where(lane_slot < MAIN, lane_slot, MAIN + lane_slot % TAIL).astype(F32)
    for part in (group, sample, code):
        part[...] = jnp.zeros_like(part)

    def step(chunk, used):
        at = pl.ds(pl.multiple_of(chunk * width, width), width)
        bag = chunk * width + iota((1, width), 1)
        group_of = (((bag >> 3) // HALF) * F + (bag & 7) + 1).astype(F32)
        sample_of = ((bag >> 3) % HALF).astype(F32)
        for k in range(owner.shape[0]):
            cold = (bags[:, at] > k) & (flag[k : k + 1, at] == 0)
            hit = (owner_ids == owner[k : k + 1, at]) & cold
            match = one_hot(hit)
            before = mxu(match, ahead, NN) + used
            place = jnp.sum(jnp.where(hit, before, 0.0), axis=0, keepdims=True)
            taken = slot_ids == place
            code_of = row_code(rows[k : k + 1, at])
            for part, value in ((group, group_of), (sample, sample_of), (code, code_of)):
                part[...] += mxu(match, jnp.where(taken, value, 0.0).astype(BF16), NT)
            used = used + jnp.sum(jnp.where(hit, 1.0, 0.0), axis=1, keepdims=True)
        return used

    lax.fori_loop(0, owner.shape[1] // width, step, jnp.zeros((owners, 1), F32))


def send_kernel(
    own, near, far, back_one, gate, group, sample, code, hot_index, out, hot_rows
):
    crossed = joined((own, near, far))
    grad = (back_one[...] * (gate[...].astype(F32).T + 1.0) + crossed).astype(BF16)
    cols, samples = grad.shape
    wide = cols // F
    row_id = iota((cols, cols), 0)
    grad = mxu(
        one_hot(iota((cols, cols), 1) == (row_id % wide) * F + row_id // wide), grad, NN
    ).astype(BF16)

    owners = group.shape[0]
    share = HOT // owners
    owner_ids = iota((owners, samples), 0)
    share_ids = iota((cols, samples), 0) // wide
    summed = jnp.zeros((owners, cols), F32)
    for f in range(F):
        copies = jnp.concatenate([grad[f * wide : (f + 1) * wide]] * share, axis=0).astype(F32)
        for k in range(hot_index.shape[0] // F):
            index = hot_index[k * F + f : k * F + f + 1, :]
            picked = jnp.where(share_ids == (index & (share - 1)), copies, 0.0).astype(BF16)
            summed += mxu(one_hot(owner_ids == (index >> 3)), picked, NT)
    hot_rows[...] = summed

    halves = jnp.concatenate(
        [grad[:, h * HALF : (h + 1) * HALF] for h in range(samples // HALF)], axis=0
    )
    groups = halves.shape[0] // wide
    sample_ids = iota((HALF, LANES), 0).astype(F32)
    tail_keep = iota((wide, MAIN), 0) // 4 == iota((wide, MAIN), 1) // TAIL
    last_row = iota((8, MAIN), 0)

    def step(o, carry):
        at = pl.ds(o, 1)
        found = mxu(halves, one_hot(sample_ids == sample[at, :]), NN)
        which = group[at, :]
        value = jnp.where(which == 1.0, found[:wide], 0.0)
        for g in range(1, groups):
            value = jnp.where(which == g + 1.0, found[g * wide : (g + 1) * wide], value)
        tail = jnp.where(tail_keep, value[:, MAIN:], 0.0)
        tail = tail[:8] + tail[8:]
        tail = tail + pltpu.roll(tail, 4, 0)
        hot = hot_rows[at, :]
        hot_hi = hot.astype(BF16).astype(F32)
        codes = code[at, :]
        last = tail
        for row, line in ((4, hot_hi), (5, hot - hot_hi), (6, codes[:, :MAIN]), (7, codes[:, MAIN:])):
            last = jnp.where(last_row == row, line, last)
        out[o] = jnp.concatenate([value[:, :MAIN], last], axis=0).astype(BF16)
        return carry

    lax.fori_loop(0, owners, step, 0, unroll=4)


def gather_kernel(got, cold, hot):
    owners = got.shape[0]
    wide = cold.shape[0]
    parts = cold.shape[1] // MAIN
    row_ids = (iota((MAIN, LANES), 0) + MAIN).astype(F32)
    part_ids = iota((parts * wide, LANES), 0) // wide
    tail_keep = iota((wide, MAIN), 0) // 4 == iota((wide, MAIN), 1) // TAIL
    low_half = iota((8, MAIN), 0) < 4

    def step(o, carry):
        total, tails = carry
        block = got[o].astype(F32)
        last = block[wide:]
        tail = jnp.where(low_half, last, pltpu.roll(last, 4, 0))
        tail = jnp.where(tail_keep, jnp.concatenate([tail, tail], axis=0), 0.0)
        values = jnp.concatenate([block[:wide], tail], axis=1)
        codes = jnp.concatenate([last[6:7], last[7:8]], axis=1)
        part = jnp.zeros(codes.shape, jnp.int32)
        lead = codes
        for p in range(1, parts):
            above = codes >= float(MAIN << p)
            part = jnp.where(above, p, part)
            lead = jnp.where(above, codes * (0.5**p), lead)
        spread = jnp.where(part_ids == part, jnp.concatenate([values] * parts, axis=0), 0.0)
        total = total + mxu(one_hot(row_ids == lead), spread.astype(BF16), NT)
        return total, tails + last

    total, tails = lax.fori_loop(
        0,
        owners,
        step,
        (jnp.zeros((MAIN, parts * wide), F32), jnp.zeros((8, MAIN), F32)),
        unroll=4,
    )
    total = total.T
    for p in range(parts):
        cold[:, p * MAIN : (p + 1) * MAIN] = total[p * wide : (p + 1) * wide]
    hot[...] = tails[4:5] + tails[5:6]


def local(
    embedded,
    gate,
    pre_hidden,
    hidden_weight,
    cross_weight,
    out_weight,
    upstream,
    hot_rows,
    cold_owner,
    cold_rows,
    hot_flag,
    bag_sizes,
):
    owners = lax.axis_size("dp")
    groups = lax.axis_size("col")
    samples, cols = embedded.shape
    inner = groups // SIDE
    total_cols = cross_weight.shape[1]
    wide = cols // F
    slots = hot_rows.shape[1]
    side = lax.axis_index("dp") % 2
    group = lax.axis_index("col")
    outer_place = jnp.stack([group // inner, side]).astype(jnp.int32)
    inner_place = jnp.stack([group % inner, side]).astype(jnp.int32)

    def shift(x, along_outer, turn):
        pairs = []
        for d in range(owners):
            for g in range(groups):
                outer, rest = divmod(g, inner)
                here = outer if along_outer else rest
                other = here ^ 1 if (d + turn) % 2 == 0 else SIDE - 1 - here
                to = other * inner + rest if along_outer else outer * inner + other
                pairs.append((d * groups + g, d * groups + to))
        return lax.ppermute(x, ("dp", "col"), pairs)

    def exchange(blocks, along_outer, beside=None):
        diagonal, near, second, own = blocks
        extra = None
        if beside is not None:
            held, diagonal = lax.optimization_barrier((beside[1], diagonal))
        first = shift(diagonal, along_outer, 0)
        near = shift(near, along_outer, 0)
        if beside is not None:
            extra = beside[0](*held)
            first, extra = lax.optimization_barrier((first, extra))
        onward = (second.astype(F32) + first.astype(F32)).astype(BF16)
        return (own, near, shift(onward, along_outer, 1)), extra

    def plan(owner, rows, flag, bags):
        return call(
            plan_kernel,
            [jax.ShapeDtypeStruct((owners, LANES), F32)] * 3,
            (owner, rows, flag, bags),
            flops=2 * 10**9,
            moved=10**7,
        )

    live = lax.broadcasted_iota(jnp.int32, hot_rows.shape, 1) < bag_sizes[:, None]
    hot_index = (
        jnp.where(live & (hot_flag == 1), hot_rows, -1)
        .T.reshape(slots, samples, F)
        .transpose(0, 2, 1)
        .reshape(slots * F, samples)
    )
    outer_rows = total_cols // SIDE

    def stage_two(terms):
        return call(
            mid_kernel,
            blocks_of(cols, samples),
            terms,
            smem=(inner_place,),
            scratch=[pltpu.VMEM((outer_rows, samples), BF16)],
            flops=4 * outer_rows * samples,
            moved=10 * outer_rows * samples,
        )

    blocks = call(
        hidden_kernel,
        blocks_of(outer_rows, samples),
        (hidden_weight, pre_hidden, upstream[:, None], out_weight[None, :]),
        smem=(outer_place,),
        flops=2 * total_cols * samples * pre_hidden.shape[1],
        moved=4 * total_cols * samples,
    )
    terms, _ = exchange(blocks, True)
    terms, routes = exchange(
        stage_two(terms), False, (plan, (cold_owner.T, cold_rows.T, hot_flag.T, bag_sizes[None, :]))
    )
    back_one, *blocks = call(
        cross_kernel,
        [jax.ShapeDtypeStruct((cols, samples), F32)] + blocks_of(outer_rows, samples),
        terms + (embedded, cross_weight),
        smem=(outer_place,),
        flops=2 * total_cols * samples * cols,
        moved=4 * total_cols * samples,
    )
    terms, _ = exchange(blocks, True)
    terms, _ = exchange(stage_two(terms), False)
    message = call(
        send_kernel,
        jax.ShapeDtypeStruct((owners, MSG_ROWS, MAIN), BF16),
        terms + (back_one, gate, *routes, hot_index),
        scratch=[pltpu.VMEM((owners, cols), F32)],
        flops=2 * 10**9,
        moved=10**7,
    )
    got = lax.all_to_all(message, "dp", split_axis=0, concat_axis=0, tiled=True)
    cold_grad, hot_sum = call(
        gather_kernel,
        [
            jax.ShapeDtypeStruct((wide, COLD_DEV), F32),
            jax.ShapeDtypeStruct((1, MAIN), F32),
        ],
        (got,),
        flops=2 * 10**9,
        moved=10**7,
    )
    hot_grad = hot_sum.reshape(HOT // owners, wide).T
    return (hot_grad, cold_grad)


def solution(mesh):
    in_specs = (
        P("dp", "col"),
        P("dp", "col"),
        P("dp", "col"),
        P(None, "col"),
        P("col", None),
        P("col"),
        P("dp"),
        P("dp", None),
        P("dp", None),
        P("dp", None),
        P("dp", None),
        P("dp"),
    )
    out_specs = (P("col", "dp"), P("col", "dp"))
    return jax.shard_map(local, mesh=mesh, in_specs=in_specs, out_specs=out_specs, check_vma=False)
```

```python
import jax
import jax.numpy as jnp
from jax import lax
from jax.experimental import pallas as pl
from jax.experimental.pallas import tpu as pltpu
from jax.sharding import PartitionSpec as P

F = 8
HOT = 512
COLD_DEV = 512
CAP = 160
SIDE = 4
MAIN = 128
TAIL = CAP - MAIN
LANES = 256
HALF = 256
MSG_ROWS = 24
F32 = jnp.float32
BF16 = jnp.bfloat16
NT = (((1,), (1,)), ((), ()))
TN = (((0,), (0,)), ((), ()))
NN = (((1,), (0,)), ((), ()))


def mxu(a, b, dims):
    return lax.dot_general(a, b, dims, preferred_element_type=F32)


def iota(shape, axis):
    return lax.broadcasted_iota(jnp.int32, shape, axis)


def one_hot(match):
    return jnp.where(match, 1.0, 0.0).astype(BF16)


def call(kernel, out_shape, inputs, smem=(), scratch=(), flops=0, moved=0):
    vmem = pl.BlockSpec(memory_space=pltpu.VMEM)
    scalar = pl.BlockSpec(memory_space=pltpu.SMEM)
    return pl.pallas_call(
        kernel,
        out_shape=out_shape,
        in_specs=[scalar] * len(smem) + [vmem] * len(inputs),
        out_specs=jax.tree.map(lambda _: vmem, out_shape),
        scratch_shapes=list(scratch),
        compiler_params=pltpu.CompilerParams(vmem_limit_bytes=40 * 2**20),
        cost_estimate=pl.CostEstimate(flops=flops, bytes_accessed=moved, transcendentals=0),
    )(*smem, *inputs)


def blocks_of(rows, lanes):
    return [jax.ShapeDtypeStruct((rows, lanes), BF16)] * 4


def partner(here, flip):
    return jnp.where(flip == 0, here ^ 1, SIDE - 1 - here)


def store_blocks(make, place, diagonal, near, second, own):
    here, side = place[0], place[1]
    for ref, block in (
        (diagonal, (here + 2) % SIDE),
        (near, partner(here, side)),
        (second, partner(here, 1 - side)),
        (own, here),
    ):
        ref[...] = make(block).astype(BF16)


def hidden_kernel(place, weight, pre_hidden, upstream, out_weight, *refs):
    slope = jnp.where(
        pre_hidden[...] > 0, upstream[...] * out_weight[...].astype(F32), 0.0
    ).astype(BF16)
    rows = refs[0].shape[0]

    def make(block):
        start = pl.multiple_of(block * rows, rows)
        return mxu(weight[pl.ds(start, rows), :], slope, NT)

    store_blocks(make, place, *refs)


def joined(terms):
    own, near, far = terms
    return own[...].astype(F32) + near[...].astype(F32) + far[...].astype(F32)


def mid_kernel(place, own, near, far, *refs):
    total = refs[4]
    total[...] = joined((own, near, far)).astype(BF16)
    rows = refs[0].shape[0]

    def make(block):
        return total[pl.ds(pl.multiple_of(block * rows, rows), rows), :]

    store_blocks(make, place, *refs[:4])


def gate_kernel(own, near, far, embedded, back_one, gated):
    total = joined((own, near, far))
    back_one[...] = total
    gated[...] = (total * embedded[...].astype(F32).T).astype(BF16)


def cross_kernel(place, w_own, w_near, w_far, w_diag, g_own, g_near, g_far, g_diag, *refs):
    total = refs[4]
    product = mxu(w_own[...], g_own[...], TN)
    for weight, gated in ((w_near, g_near), (w_far, g_far), (w_diag, g_diag)):
        product += mxu(weight[...], gated[...], TN)
    total[...] = product.astype(BF16)
    rows = refs[0].shape[0]

    def make(block):
        return total[pl.ds(pl.multiple_of(block * rows, rows), rows), :]

    store_blocks(make, place, *refs[:4])


def row_code(row):
    return ((MAIN + (row & (MAIN - 1))) << (row >> 7)).astype(F32)


def plan_kernel(place, owner, rows, flag, bags, weight, group, sample, code, *blocks):
    span = blocks[0].shape[1]

    def make(block):
        return weight[:, pl.ds(pl.multiple_of(block * span, span), span)]

    store_blocks(make, place, *blocks)
    width = 512
    owners = group.shape[0]
    ahead = one_hot(iota((width, width), 0) < iota((width, width), 1))
    owner_ids = iota((owners, width), 0)
    lane_slot = iota((LANES, width), 0)
    slot_ids = jnp.where(lane_slot < MAIN, lane_slot, MAIN + lane_slot % TAIL).astype(F32)
    for part in (group, sample, code):
        part[...] = jnp.zeros_like(part)

    def step(chunk, used):
        at = pl.ds(pl.multiple_of(chunk * width, width), width)
        bag = chunk * width + iota((1, width), 1)
        group_of = (((bag >> 3) // HALF) * F + (bag & 7) + 1).astype(F32)
        sample_of = ((bag >> 3) % HALF).astype(F32)
        for k in range(owner.shape[0]):
            cold = (bags[:, at] > k) & (flag[k : k + 1, at] == 0)
            hit = (owner_ids == owner[k : k + 1, at]) & cold
            match = one_hot(hit)
            before = mxu(match, ahead, NN) + used
            place = jnp.sum(jnp.where(hit, before, 0.0), axis=0, keepdims=True)
            taken = slot_ids == place
            code_of = row_code(rows[k : k + 1, at])
            for part, value in ((group, group_of), (sample, sample_of), (code, code_of)):
                part[...] += mxu(match, jnp.where(taken, value, 0.0).astype(BF16), NT)
            used = used + jnp.sum(jnp.where(hit, 1.0, 0.0), axis=1, keepdims=True)
        return used

    lax.fori_loop(0, owner.shape[1] // width, step, jnp.zeros((owners, 1), F32))


def send_kernel(
    own, near, far, back_one, gate, group, sample, code, hot_index, out, hot_rows
):
    crossed = joined((own, near, far))
    grad = (back_one[...] * (gate[...].astype(F32).T + 1.0) + crossed).astype(BF16)
    cols, samples = grad.shape
    wide = cols // F
    row_id = iota((cols, cols), 0)
    grad = mxu(
        one_hot(iota((cols, cols), 1) == (row_id % wide) * F + row_id // wide), grad, NN
    ).astype(BF16)

    owners = group.shape[0]
    share = HOT // owners
    owner_ids = iota((owners, samples), 0)
    share_ids = iota((cols, samples), 0) // wide
    summed = jnp.zeros((owners, cols), F32)
    for f in range(F):
        copies = jnp.concatenate([grad[f * wide : (f + 1) * wide]] * share, axis=0).astype(F32)
        for k in range(hot_index.shape[0] // F):
            index = hot_index[k * F + f : k * F + f + 1, :]
            picked = jnp.where(share_ids == (index & (share - 1)), copies, 0.0).astype(BF16)
            summed += mxu(one_hot(owner_ids == (index >> 3)), picked, NT)
    hot_rows[...] = summed

    halves = jnp.concatenate(
        [grad[:, h * HALF : (h + 1) * HALF] for h in range(samples // HALF)], axis=0
    )
    groups = halves.shape[0] // wide
    sample_ids = iota((HALF, LANES), 0).astype(F32)
    tail_keep = iota((wide, MAIN), 0) // 4 == iota((wide, MAIN), 1) // TAIL
    last_row = iota((8, MAIN), 0)

    def step(o, carry):
        at = pl.ds(o, 1)
        found = mxu(halves, one_hot(sample_ids == sample[at, :]), NN)
        which = group[at, :]
        value = jnp.where(which == 1.0, found[:wide], 0.0)
        for g in range(1, groups):
            value = jnp.where(which == g + 1.0, found[g * wide : (g + 1) * wide], value)
        tail = jnp.where(tail_keep, value[:, MAIN:], 0.0)
        tail = tail[:8] + tail[8:]
        tail = tail + pltpu.roll(tail, 4, 0)
        hot = hot_rows[at, :]
        hot_hi = hot.astype(BF16).astype(F32)
        codes = code[at, :]
        last = tail
        for row, line in ((4, hot_hi), (5, hot - hot_hi), (6, codes[:, :MAIN]), (7, codes[:, MAIN:])):
            last = jnp.where(last_row == row, line, last)
        out[o] = jnp.concatenate([value[:, :MAIN], last], axis=0).astype(BF16)
        return carry

    lax.fori_loop(0, owners, step, 0, unroll=4)


def gather_kernel(got, cold, hot):
    owners = got.shape[0]
    wide = cold.shape[0]
    parts = cold.shape[1] // MAIN
    row_ids = (iota((MAIN, LANES), 0) + MAIN).astype(F32)
    part_ids = iota((parts * wide, LANES), 0) // wide
    tail_keep = iota((wide, MAIN), 0) // 4 == iota((wide, MAIN), 1) // TAIL
    low_half = iota((8, MAIN), 0) < 4

    def step(o, carry):
        total, tails = carry
        block = got[o].astype(F32)
        last = block[wide:]
        tail = jnp.where(low_half, last, pltpu.roll(last, 4, 0))
        tail = jnp.where(tail_keep, jnp.concatenate([tail, tail], axis=0), 0.0)
        values = jnp.concatenate([block[:wide], tail], axis=1)
        codes = jnp.concatenate([last[6:7], last[7:8]], axis=1)
        part = jnp.zeros(codes.shape, jnp.int32)
        lead = codes
        for p in range(1, parts):
            above = codes >= float(MAIN << p)
            part = jnp.where(above, p, part)
            lead = jnp.where(above, codes * (0.5**p), lead)
        spread = jnp.where(part_ids == part, jnp.concatenate([values] * parts, axis=0), 0.0)
        total = total + mxu(one_hot(row_ids == lead), spread.astype(BF16), NT)
        return total, tails + last

    total, tails = lax.fori_loop(
        0,
        owners,
        step,
        (jnp.zeros((MAIN, parts * wide), F32), jnp.zeros((8, MAIN), F32)),
        unroll=4,
    )
    total = total.T
    for p in range(parts):
        cold[:, p * MAIN : (p + 1) * MAIN] = total[p * wide : (p + 1) * wide]
    hot[...] = tails[4:5] + tails[5:6]


def local(
    embedded,
    gate,
    pre_hidden,
    hidden_weight,
    cross_weight,
    out_weight,
    upstream,
    hot_rows,
    cold_owner,
    cold_rows,
    hot_flag,
    bag_sizes,
):
    owners = lax.axis_size("dp")
    groups = lax.axis_size("col")
    samples, cols = embedded.shape
    inner = groups // SIDE
    total_cols = cross_weight.shape[1]
    wide = cols // F
    slots = hot_rows.shape[1]
    side = lax.axis_index("dp") % 2
    group = lax.axis_index("col")
    outer_place = jnp.stack([group // inner, side]).astype(jnp.int32)
    inner_place = jnp.stack([group % inner, side]).astype(jnp.int32)

    outer_rows = total_cols // SIDE

    def shift(x, along_outer, turn):
        pairs = []
        for d in range(owners):
            for g in range(groups):
                outer, rest = divmod(g, inner)
                here = outer if along_outer else rest
                if turn is None:
                    other = (here + 2) % SIDE
                else:
                    other = here ^ 1 if (d + turn) % 2 == 0 else SIDE - 1 - here
                to = other * inner + rest if along_outer else outer * inner + other
                pairs.append((d * groups + g, d * groups + to))
        return lax.ppermute(x, ("dp", "col"), pairs)

    def onward(second, first):
        return (second.astype(F32) + first.astype(F32)).astype(BF16)

    def exchange(blocks, along_outer):
        diagonal, near, second, own = blocks
        first = shift(diagonal, along_outer, 0)
        near = shift(near, along_outer, 0)
        return own, near, shift(onward(second, first), along_outer, 1)

    def exchange_beside(blocks, held):
        diagonal, near, second, own = blocks
        held, diagonal = lax.optimization_barrier((held, diagonal))
        first = shift(diagonal, False, 0)
        near = shift(near, False, 0)
        *routes, w_diag, w_near, w_far, w_own = call(
            plan_kernel,
            [jax.ShapeDtypeStruct((owners, LANES), F32)] * 3 + blocks_of(cols, outer_rows),
            held,
            smem=(outer_place,),
            flops=2 * 10**9,
            moved=10**7,
        )
        first, routes, parts = lax.optimization_barrier((first, routes, (w_near, w_far, w_diag)))
        far = onward(second, first)
        far, parts = lax.optimization_barrier((far, parts))
        far = shift(far, False, 1)
        near, parts = lax.optimization_barrier((near, parts))
        parts = tuple(shift(part, True, turn) for part, turn in zip(parts, (0, 1, None)))
        far, parts = lax.optimization_barrier((far, parts))
        return (own, near, far), routes, (w_own, *parts)

    live = lax.broadcasted_iota(jnp.int32, hot_rows.shape, 1) < bag_sizes[:, None]
    hot_index = (
        jnp.where(live & (hot_flag == 1), hot_rows, -1)
        .T.reshape(slots, samples, F)
        .transpose(0, 2, 1)
        .reshape(slots * F, samples)
    )

    def stage_two(terms):
        return call(
            mid_kernel,
            blocks_of(cols, samples),
            terms,
            smem=(inner_place,),
            scratch=[pltpu.VMEM((outer_rows, samples), BF16)],
            flops=4 * outer_rows * samples,
            moved=10 * outer_rows * samples,
        )

    blocks = call(
        hidden_kernel,
        blocks_of(outer_rows, samples),
        (hidden_weight, pre_hidden, upstream[:, None], out_weight[None, :]),
        smem=(outer_place,),
        flops=2 * total_cols * samples * pre_hidden.shape[1],
        moved=4 * total_cols * samples,
    )
    terms, routes, weights = exchange_beside(
        stage_two(exchange(blocks, True)),
        (cold_owner.T, cold_rows.T, hot_flag.T, bag_sizes[None, :], cross_weight),
    )
    back_one, gated = call(
        gate_kernel,
        [jax.ShapeDtypeStruct((cols, samples), F32), jax.ShapeDtypeStruct((cols, samples), BF16)],
        terms + (embedded,),
        flops=4 * cols * samples,
        moved=16 * cols * samples,
    )
    near = shift(gated, True, 0)
    far = shift(gated, True, 1)
    diagonal = shift(near, True, 1)
    blocks = call(
        cross_kernel,
        blocks_of(cols, samples),
        weights + (gated, near, far, diagonal),
        smem=(inner_place,),
        scratch=[pltpu.VMEM((outer_rows, samples), BF16)],
        flops=2 * total_cols * samples * cols,
        moved=4 * outer_rows * samples,
    )
    terms = exchange(blocks, False)
    message = call(
        send_kernel,
        jax.ShapeDtypeStruct((owners, MSG_ROWS, MAIN), BF16),
        terms + (back_one, gate, *routes, hot_index),
        scratch=[pltpu.VMEM((owners, cols), F32)],
        flops=2 * 10**9,
        moved=10**7,
    )
    got = lax.all_to_all(message, "dp", split_axis=0, concat_axis=0, tiled=True)
    cold_grad, hot_sum = call(
        gather_kernel,
        [
            jax.ShapeDtypeStruct((wide, COLD_DEV), F32),
            jax.ShapeDtypeStruct((1, MAIN), F32),
        ],
        (got,),
        flops=2 * 10**9,
        moved=10**7,
    )
    hot_grad = hot_sum.reshape(HOT // owners, wide).T
    return (hot_grad, cold_grad)


def solution(mesh):
    in_specs = (
        P("dp", "col"),
        P("dp", "col"),
        P("dp", "col"),
        P(None, "col"),
        P("col", None),
        P("col"),
        P("dp"),
        P("dp", None),
        P("dp", None),
        P("dp", None),
        P("dp", None),
        P("dp"),
    )
    out_specs = (P("col", "dp"), P("col", "dp"))
    return jax.shard_map(local, mesh=mesh, in_specs=in_specs, out_specs=out_specs, check_vma=False)
```

```python
import functools

import jax
import jax.numpy as jnp
from jax import lax
from jax.experimental import pallas as pl
from jax.experimental.pallas import tpu as pltpu
from jax.sharding import PartitionSpec as P

F = 8
HOT = 512
COLD_DEV = 512
CAP = 160
SIDE = 4
MAIN = 128
TAIL = CAP - MAIN
LANES = 256
HALF = 256
MSG_ROWS = 24
F32 = jnp.float32
BF16 = jnp.bfloat16
NT = (((1,), (1,)), ((), ()))
TN = (((0,), (0,)), ((), ()))
NN = (((1,), (0,)), ((), ()))


def mxu(a, b, dims):
    return lax.dot_general(a, b, dims, preferred_element_type=F32)


def iota(shape, axis):
    return lax.broadcasted_iota(jnp.int32, shape, axis)


def one_hot(match):
    return jnp.where(match, 1.0, 0.0).astype(BF16)


def call(kernel, out_shape, inputs, smem=(), scratch=(), flops=0, moved=0):
    vmem = pl.BlockSpec(memory_space=pltpu.VMEM)
    scalar = pl.BlockSpec(memory_space=pltpu.SMEM)
    return pl.pallas_call(
        kernel,
        out_shape=out_shape,
        in_specs=[scalar] * len(smem) + [vmem] * len(inputs),
        out_specs=jax.tree.map(lambda _: vmem, out_shape),
        scratch_shapes=list(scratch),
        compiler_params=pltpu.CompilerParams(vmem_limit_bytes=40 * 2**20),
        cost_estimate=pl.CostEstimate(flops=flops, bytes_accessed=moved, transcendentals=0),
    )(*smem, *inputs)


def blocks_of(rows, lanes):
    return [jax.ShapeDtypeStruct((rows, lanes), BF16)] * 4


def partner(here, flip):
    return jnp.where(flip == 0, here ^ 1, SIDE - 1 - here)


def store_blocks(make, place, diagonal, near, second, own):
    here, side = place[0], place[1]
    for ref, block in (
        (diagonal, (here + 2) % SIDE),
        (near, partner(here, side)),
        (second, partner(here, 1 - side)),
        (own, here),
    ):
        ref[...] = make(block).astype(BF16)


def hidden_kernel(place, weight, pre_hidden, upstream, out_weight, *refs):
    scale = jnp.broadcast_to(upstream[...], (8, upstream.shape[1])).T[:, :1]
    slope = jnp.where(
        pre_hidden[...] > 0, scale * out_weight[...].astype(F32), 0.0
    ).astype(BF16)
    rows = refs[0].shape[0]

    def make(block):
        start = pl.multiple_of(block * rows, rows)
        return mxu(weight[pl.ds(start, rows), :], slope, NT)

    store_blocks(make, place, *refs)


def joined(terms):
    own, near, far = terms
    return own[...].astype(F32) + near[...].astype(F32) + far[...].astype(F32)


def mid_kernel(place, outer_place, own, near, far, weight, *refs):
    total = refs[8]
    total[...] = joined((own, near, far)).astype(BF16)
    rows = refs[0].shape[0]

    def make(block):
        return total[pl.ds(pl.multiple_of(block * rows, rows), rows), :]

    store_blocks(make, place, *refs[:4])
    span = refs[4].shape[1]

    def weight_block(block):
        return weight[:, pl.ds(pl.multiple_of(block * span, span), span)]

    store_blocks(weight_block, outer_place, *refs[4:8])


def gate_kernel(own, near, far, embedded, back_one, gated):
    total = joined((own, near, far))
    back_one[...] = total
    gated[...] = (total * embedded[...].astype(F32).T).astype(BF16)


def cross_kernel(place, w_own, w_near, w_far, w_diag, g_own, g_near, g_far, g_diag, *refs):
    total = refs[4]
    product = mxu(w_own[...], g_own[...], TN)
    for weight, gated in ((w_near, g_near), (w_far, g_far), (w_diag, g_diag)):
        product += mxu(weight[...], gated[...], TN)
    total[...] = product.astype(BF16)
    rows = refs[0].shape[0]

    def make(block):
        return total[pl.ds(pl.multiple_of(block * rows, rows), rows), :]

    store_blocks(make, place, *refs[:4])


def row_code(row):
    return ((MAIN + (row & (MAIN - 1))) << (row >> 7)).astype(F32)


def plan_kernel(begin, end, owner, rows, flag, bags, *refs):
    width = 512
    before_parts, outs, parts = (refs[:4], refs[4:7], refs[7:]) if begin else ((), (), refs)
    owners = parts[0].shape[0]
    ahead = one_hot(iota((width, width), 0) < iota((width, width), 1))
    owner_ids = iota((owners, width), 0)
    slot_ids = iota((CAP, width), 0).astype(F32)
    for i, part in enumerate(parts):
        part[...] = before_parts[i][...] if begin else jnp.zeros_like(part)

    def step(chunk, used):
        at = pl.ds(pl.multiple_of(chunk * width, width), width)
        bag = chunk * width + iota((1, width), 1)
        group_of = (((bag >> 3) // HALF) * F + (bag & 7) + 1).astype(F32)
        sample_of = ((bag >> 3) % HALF).astype(F32)
        for k in range(owner.shape[0]):
            cold = (bags[:, at] > k) & (flag[k : k + 1, at] == 0)
            hit = (owner_ids == owner[k : k + 1, at]) & cold
            match = one_hot(hit)
            before = mxu(match, ahead, NN) + used
            place = jnp.sum(jnp.where(hit, before, 0.0), axis=0, keepdims=True)
            taken = slot_ids == place
            code_of = row_code(rows[k : k + 1, at])
            for part, value in zip(parts, (group_of, sample_of, code_of)):
                part[...] += mxu(match, jnp.where(taken, value, 0.0).astype(BF16), NT)
            used = used + jnp.sum(jnp.where(hit, 1.0, 0.0), axis=1, keepdims=True)
        return used

    used = lax.fori_loop(begin, end, step, parts[3][:, :1])
    parts[3][...] = jnp.broadcast_to(used, parts[3].shape)
    for out, part in zip(outs, parts):
        out[:, :MAIN] = part[:, :MAIN]
        out[:, MAIN:] = jnp.concatenate([part[:, MAIN:]] * (MAIN // TAIL), axis=1)


def send_kernel(
    own, near, far, back_one, gate, group, sample, code, hot_index, out, hot_rows
):
    crossed = joined((own, near, far))
    grad = (back_one[...] * (gate[...].astype(F32).T + 1.0) + crossed).astype(BF16)
    cols, samples = grad.shape
    wide = cols // F
    row_id = iota((cols, cols), 0)
    grad = mxu(
        one_hot(iota((cols, cols), 1) == (row_id % wide) * F + row_id // wide), grad, NN
    ).astype(BF16)

    owners = group.shape[0]
    share = HOT // owners
    owner_ids = iota((owners, samples), 0)
    share_ids = iota((cols, samples), 0) // wide
    summed = jnp.zeros((owners, cols), F32)
    for f in range(F):
        copies = jnp.concatenate([grad[f * wide : (f + 1) * wide]] * share, axis=0).astype(F32)
        for k in range(hot_index.shape[0] // F):
            index = hot_index[k * F + f : k * F + f + 1, :]
            picked = jnp.where(share_ids == (index & (share - 1)), copies, 0.0).astype(BF16)
            summed += mxu(one_hot(owner_ids == (index >> 3)), picked, NT)
    hot_rows[...] = summed

    halves = jnp.concatenate(
        [grad[:, h * HALF : (h + 1) * HALF] for h in range(samples // HALF)], axis=0
    )
    groups = halves.shape[0] // wide
    sample_ids = iota((HALF, LANES), 0).astype(F32)
    tail_keep = iota((wide, MAIN), 0) // 4 == iota((wide, MAIN), 1) // TAIL
    last_row = iota((8, MAIN), 0)

    def step(o, carry):
        at = pl.ds(o, 1)
        found = mxu(halves, one_hot(sample_ids == sample[at, :]), NN)
        which = group[at, :]
        value = jnp.where(which == 1.0, found[:wide], 0.0)
        for g in range(1, groups):
            value = jnp.where(which == g + 1.0, found[g * wide : (g + 1) * wide], value)
        tail = jnp.where(tail_keep, value[:, MAIN:], 0.0)
        tail = tail[:8] + tail[8:]
        tail = tail + pltpu.roll(tail, 4, 0)
        hot = hot_rows[at, :]
        hot_hi = hot.astype(BF16).astype(F32)
        codes = code[at, :]
        last = tail
        for row, line in ((4, hot_hi), (5, hot - hot_hi), (6, codes[:, :MAIN]), (7, codes[:, MAIN:])):
            last = jnp.where(last_row == row, line, last)
        out[o] = jnp.concatenate([value[:, :MAIN], last], axis=0).astype(BF16)
        return carry

    lax.fori_loop(0, owners, step, 0, unroll=4)


def gather_kernel(got, cold, hot):
    owners = got.shape[0]
    wide = cold.shape[0]
    parts = cold.shape[1] // MAIN
    row_ids = (iota((MAIN, LANES), 0) + MAIN).astype(F32)
    part_ids = iota((parts * wide, LANES), 0) // wide
    tail_keep = iota((wide, MAIN), 0) // 4 == iota((wide, MAIN), 1) // TAIL
    low_half = iota((8, MAIN), 0) < 4

    def step(o, carry):
        total, tails = carry
        block = got[o].astype(F32)
        last = block[wide:]
        tail = jnp.where(low_half, last, pltpu.roll(last, 4, 0))
        tail = jnp.where(tail_keep, jnp.concatenate([tail, tail], axis=0), 0.0)
        values = jnp.concatenate([block[:wide], tail], axis=1)
        codes = jnp.concatenate([last[6:7], last[7:8]], axis=1)
        part = jnp.zeros(codes.shape, jnp.int32)
        lead = codes
        for p in range(1, parts):
            above = codes >= float(MAIN << p)
            part = jnp.where(above, p, part)
            lead = jnp.where(above, codes * (0.5**p), lead)
        spread = jnp.where(part_ids == part, jnp.concatenate([values] * parts, axis=0), 0.0)
        total = total + mxu(one_hot(row_ids == lead), spread.astype(BF16), NT)
        return total, tails + last

    total, tails = lax.fori_loop(
        0,
        owners,
        step,
        (jnp.zeros((MAIN, parts * wide), F32), jnp.zeros((8, MAIN), F32)),
        unroll=4,
    )
    total = total.T
    for p in range(parts):
        cold[:, p * MAIN : (p + 1) * MAIN] = total[p * wide : (p + 1) * wide]
    hot[...] = tails[4:5] + tails[5:6]


def local(
    embedded,
    gate,
    pre_hidden,
    hidden_weight,
    cross_weight,
    out_weight,
    upstream,
    hot_rows,
    cold_owner,
    cold_rows,
    hot_flag,
    bag_sizes,
):
    owners = lax.axis_size("dp")
    groups = lax.axis_size("col")
    samples, cols = embedded.shape
    inner = groups // SIDE
    total_cols = cross_weight.shape[1]
    wide = cols // F
    slots = hot_rows.shape[1]
    side = lax.axis_index("dp") % 2
    group = lax.axis_index("col")
    outer_place = jnp.stack([group // inner, side]).astype(jnp.int32)
    inner_place = jnp.stack([group % inner, side]).astype(jnp.int32)

    outer_rows = total_cols // SIDE

    def shift(x, along_outer, turn):
        pairs = []
        for d in range(owners):
            for g in range(groups):
                outer, rest = divmod(g, inner)
                here = outer if along_outer else rest
                if turn is None:
                    other = (here + 2) % SIDE
                else:
                    other = here ^ 1 if (d + turn) % 2 == 0 else SIDE - 1 - here
                to = other * inner + rest if along_outer else outer * inner + other
                pairs.append((d * groups + g, d * groups + to))
        return lax.ppermute(x, ("dp", "col"), pairs)

    def onward(second, first):
        return (second.astype(F32) + first.astype(F32)).astype(BF16)

    def exchange(blocks, along_outer, work=None, held=(), parts=()):
        diagonal, near, second, own = blocks
        if work is not None:
            held, diagonal = lax.optimization_barrier((held, diagonal))
        first = shift(diagonal, along_outer, 0)
        near = shift(near, along_outer, 0)
        parts = tuple(shift(part, True, turn) for part, turn in zip(parts, (0, 1, None)))
        done = ()
        if work is not None:
            done = tuple(work(held))
            first, done, parts = lax.optimization_barrier((first, done, parts))
        return (own, near, shift(onward(second, first), along_outer, 1)), done, parts

    state = [jax.ShapeDtypeStruct((owners, CAP), F32)] * 3
    state += [jax.ShapeDtypeStruct((owners, MAIN), F32)]
    chunks = cold_owner.shape[0] // 512

    def plan(begin, end, out_shape, scratch=()):
        return lambda held: call(
            functools.partial(plan_kernel, begin, end),
            out_shape,
            held,
            scratch=scratch,
            flops=5 * 10**8,
            moved=0,
        )

    routing = [jax.ShapeDtypeStruct((owners, LANES), F32)] * 3
    slots_in = (cold_owner.T, cold_rows.T, hot_flag.T, bag_sizes[None, :])
    live = lax.broadcasted_iota(jnp.int32, hot_rows.shape, 1) < bag_sizes[:, None]
    hot_index = (
        jnp.where(live & (hot_flag == 1), hot_rows, -1)
        .T.reshape(slots, samples, F)
        .transpose(0, 2, 1)
        .reshape(slots * F, samples)
    )

    def stage_two(terms):
        return call(
            mid_kernel,
            blocks_of(cols, samples) + blocks_of(cols, outer_rows),
            terms + (cross_weight,),
            smem=(inner_place, outer_place),
            scratch=[pltpu.VMEM((outer_rows, samples), BF16)],
            flops=4 * outer_rows * samples,
            moved=10 * outer_rows * samples,
        )

    blocks = call(
        hidden_kernel,
        blocks_of(outer_rows, samples),
        (hidden_weight, pre_hidden, upstream[None, :], out_weight[None, :]),
        smem=(outer_place,),
        flops=2 * total_cols * samples * pre_hidden.shape[1],
        moved=4 * total_cols * samples,
    )
    terms, _, _ = exchange(blocks, True)
    *blocks, w_diag, w_near, w_far, w_own = stage_two(terms)
    terms, planned, parts = exchange(
        blocks, False, plan(0, chunks // 2, state), slots_in, (w_near, w_far, w_diag)
    )
    weights = (w_own, *parts)
    back_one, gated = call(
        gate_kernel,
        [jax.ShapeDtypeStruct((cols, samples), F32), jax.ShapeDtypeStruct((cols, samples), BF16)],
        terms + (embedded,),
        flops=4 * cols * samples,
        moved=16 * cols * samples,
    )
    near = shift(gated, True, 0)
    far = shift(gated, True, 1)
    diagonal = shift(near, True, 1)
    blocks = call(
        cross_kernel,
        blocks_of(cols, samples),
        weights + (gated, near, far, diagonal),
        smem=(inner_place,),
        scratch=[pltpu.VMEM((outer_rows, samples), BF16)],
        flops=2 * total_cols * samples * cols,
        moved=4 * outer_rows * samples,
    )
    terms, routes, _ = exchange(
        blocks, False, plan(chunks // 2, chunks, routing, [pltpu.VMEM(x.shape, F32) for x in state]), slots_in + planned
    )
    message = call(
        send_kernel,
        jax.ShapeDtypeStruct((owners, MSG_ROWS, MAIN), BF16),
        terms + (back_one, gate, *routes, hot_index),
        scratch=[pltpu.VMEM((owners, cols), F32)],
        flops=2 * 10**9,
        moved=10**7,
    )
    got = lax.all_to_all(message, "dp", split_axis=0, concat_axis=0, tiled=True)
    cold_grad, hot_sum = call(
        gather_kernel,
        [
            jax.ShapeDtypeStruct((wide, COLD_DEV), F32),
            jax.ShapeDtypeStruct((1, MAIN), F32),
        ],
        (got,),
        flops=2 * 10**9,
        moved=10**7,
    )
    hot_grad = hot_sum.reshape(HOT // owners, wide).T
    return (hot_grad, cold_grad)


def solution(mesh):
    in_specs = (
        P("dp", "col"),
        P("dp", "col"),
        P("dp", "col"),
        P(None, "col"),
        P("col", None),
        P("col"),
        P("dp"),
        P("dp", None),
        P("dp", None),
        P("dp", None),
        P("dp", None),
        P("dp"),
    )
    out_specs = (P("col", "dp"), P("col", "dp"))
    return jax.shard_map(local, mesh=mesh, in_specs=in_specs, out_specs=out_specs, check_vma=False)
```

```python
import functools

import jax
import jax.numpy as jnp
from jax import lax
from jax.experimental import pallas as pl
from jax.experimental.pallas import tpu as pltpu
from jax.sharding import PartitionSpec as P

F = 8
HOT = 512
COLD_DEV = 512
CAP = 160
SIDE = 4
MAIN = 128
TAIL = CAP - MAIN
LANES = 256
HALF = 256
MSG_ROWS = 24
F32 = jnp.float32
BF16 = jnp.bfloat16
NT = (((1,), (1,)), ((), ()))
TN = (((0,), (0,)), ((), ()))
NN = (((1,), (0,)), ((), ()))


def mxu(a, b, dims):
    return lax.dot_general(a, b, dims, preferred_element_type=F32)


def iota(shape, axis):
    return lax.broadcasted_iota(jnp.int32, shape, axis)


def one_hot(match):
    return jnp.where(match, 1.0, 0.0).astype(BF16)


def call(kernel, out_shape, inputs, smem=(), scratch=(), flops=0, moved=0):
    vmem = pl.BlockSpec(memory_space=pltpu.VMEM)
    scalar = pl.BlockSpec(memory_space=pltpu.SMEM)
    return pl.pallas_call(
        kernel,
        out_shape=out_shape,
        in_specs=[scalar] * len(smem) + [vmem] * len(inputs),
        out_specs=jax.tree.map(lambda _: vmem, out_shape),
        scratch_shapes=list(scratch),
        compiler_params=pltpu.CompilerParams(vmem_limit_bytes=40 * 2**20),
        cost_estimate=pl.CostEstimate(flops=flops, bytes_accessed=moved, transcendentals=0),
    )(*smem, *inputs)


def blocks_of(rows, lanes):
    return [jax.ShapeDtypeStruct((rows, lanes), BF16)] * 4


def partner(here, flip):
    return jnp.where(flip == 0, here ^ 1, SIDE - 1 - here)


def store_blocks(make, place, diagonal, near, second, own):
    here, side = place[0], place[1]
    for ref, block in (
        (diagonal, (here + 2) % SIDE),
        (near, partner(here, side)),
        (second, partner(here, 1 - side)),
        (own, here),
    ):
        ref[...] = make(block).astype(BF16)


def hidden_kernel(place, weight, pre_hidden, upstream, out_weight, *refs):
    scale = jnp.broadcast_to(upstream[...], (8, upstream.shape[1])).T[:, :1]
    slope = jnp.where(
        pre_hidden[...] > 0, scale * out_weight[...].astype(F32), 0.0
    ).astype(BF16)
    rows = refs[0].shape[0]

    def make(block):
        start = pl.multiple_of(block * rows, rows)
        return mxu(weight[pl.ds(start, rows), :], slope, NT)

    store_blocks(make, place, *refs)


def joined(terms):
    own, near, far = terms
    return own[...].astype(F32) + near[...].astype(F32) + far[...].astype(F32)


def mid_kernel(place, outer_place, own, near, far, weight, *refs):
    total = refs[8]
    total[...] = joined((own, near, far)).astype(BF16)
    rows = refs[0].shape[0]

    def make(block):
        return total[pl.ds(pl.multiple_of(block * rows, rows), rows), :]

    store_blocks(make, place, *refs[:4])
    span = refs[4].shape[1]

    def weight_block(block):
        return weight[:, pl.ds(pl.multiple_of(block * span, span), span)]

    store_blocks(weight_block, outer_place, *refs[4:8])


def gate_kernel(own, near, far, embedded, back_one, gated):
    total = joined((own, near, far))
    back_one[...] = total
    gated[...] = (total * embedded[...].astype(F32).T).astype(BF16)


def cross_kernel(place, w_own, w_diag, w_near, w_far, g_own, g_diag, g_near, g_far, *refs):
    total = refs[4]
    product = mxu(w_own[...], g_own[...], TN)
    for weight, gated in ((w_near, g_near), (w_far, g_far), (w_diag, g_diag)):
        product += mxu(weight[...], gated[...], TN)
    total[...] = product.astype(BF16)
    rows = refs[0].shape[0]

    def make(block):
        return total[pl.ds(pl.multiple_of(block * rows, rows), rows), :]

    store_blocks(make, place, *refs[:4])


def row_code(row):
    return ((MAIN + (row & (MAIN - 1))) << (row >> 7)).astype(F32)


def plan_kernel(begin, end, owner, rows, flag, bags, *refs):
    width = 512
    before_parts, outs, parts = (refs[:4], refs[4:7], refs[7:]) if begin else ((), (), refs)
    owners = parts[0].shape[0]
    ahead = one_hot(iota((width, width), 0) < iota((width, width), 1))
    owner_ids = iota((owners, width), 0)
    slot_ids = iota((CAP, width), 0).astype(F32)
    for i, part in enumerate(parts):
        part[...] = before_parts[i][...] if begin else jnp.zeros_like(part)

    def step(chunk, used):
        at = pl.ds(pl.multiple_of(chunk * width, width), width)
        bag = chunk * width + iota((1, width), 1)
        group_of = (((bag >> 3) // HALF) * F + (bag & 7) + 1).astype(F32)
        sample_of = ((bag >> 3) % HALF).astype(F32)
        for k in range(owner.shape[0]):
            cold = (bags[:, at] > k) & (flag[k : k + 1, at] == 0)
            hit = (owner_ids == owner[k : k + 1, at]) & cold
            match = one_hot(hit)
            before = mxu(match, ahead, NN) + used
            place = jnp.sum(jnp.where(hit, before, 0.0), axis=0, keepdims=True)
            taken = slot_ids == place
            code_of = row_code(rows[k : k + 1, at])
            for part, value in zip(parts, (group_of, sample_of, code_of)):
                part[...] += mxu(match, jnp.where(taken, value, 0.0).astype(BF16), NT)
            used = used + jnp.sum(jnp.where(hit, 1.0, 0.0), axis=1, keepdims=True)
        return used

    used = lax.fori_loop(begin, end, step, parts[3][:, :1])
    parts[3][...] = jnp.broadcast_to(used, parts[3].shape)
    for out, part in zip(outs, parts):
        out[:, :MAIN] = part[:, :MAIN]
        out[:, MAIN:] = jnp.concatenate([part[:, MAIN:]] * (MAIN // TAIL), axis=1)


def send_kernel(
    own, near, far, back_one, gate, group, sample, code, hot_index, out, hot_rows
):
    crossed = joined((own, near, far))
    grad = (back_one[...] * (gate[...].astype(F32).T + 1.0) + crossed).astype(BF16)
    cols, samples = grad.shape
    wide = cols // F
    row_id = iota((cols, cols), 0)
    grad = mxu(
        one_hot(iota((cols, cols), 1) == (row_id % wide) * F + row_id // wide), grad, NN
    ).astype(BF16)

    owners = group.shape[0]
    share = HOT // owners
    owner_ids = iota((owners, samples), 0)
    share_ids = iota((cols, samples), 0) // wide
    summed = jnp.zeros((owners, cols), F32)
    for f in range(F):
        copies = jnp.concatenate([grad[f * wide : (f + 1) * wide]] * share, axis=0).astype(F32)
        for k in range(hot_index.shape[0] // F):
            index = hot_index[k * F + f : k * F + f + 1, :]
            picked = jnp.where(share_ids == (index & (share - 1)), copies, 0.0).astype(BF16)
            summed += mxu(one_hot(owner_ids == (index >> 3)), picked, NT)
    hot_rows[...] = summed

    halves = jnp.concatenate(
        [grad[:, h * HALF : (h + 1) * HALF] for h in range(samples // HALF)], axis=0
    )
    groups = halves.shape[0] // wide
    sample_ids = iota((HALF, LANES), 0).astype(F32)
    tail_keep = iota((wide, MAIN), 0) // 4 == iota((wide, MAIN), 1) // TAIL
    last_row = iota((8, MAIN), 0)

    def step(o, carry):
        at = pl.ds(o, 1)
        found = mxu(halves, one_hot(sample_ids == sample[at, :]), NN)
        which = group[at, :]
        value = jnp.where(which == 1.0, found[:wide], 0.0)
        for g in range(1, groups):
            value = jnp.where(which == g + 1.0, found[g * wide : (g + 1) * wide], value)
        tail = jnp.where(tail_keep, value[:, MAIN:], 0.0)
        tail = tail[:8] + tail[8:]
        tail = tail + pltpu.roll(tail, 4, 0)
        hot = hot_rows[at, :]
        hot_hi = hot.astype(BF16).astype(F32)
        codes = code[at, :]
        last = tail
        for row, line in ((4, hot_hi), (5, hot - hot_hi), (6, codes[:, :MAIN]), (7, codes[:, MAIN:])):
            last = jnp.where(last_row == row, line, last)
        out[o] = jnp.concatenate([value[:, :MAIN], last], axis=0).astype(BF16)
        return carry

    lax.fori_loop(0, owners, step, 0, unroll=8)


def gather_kernel(got, cold, hot):
    owners = got.shape[0]
    wide = cold.shape[0]
    parts = cold.shape[1] // MAIN
    row_ids = (iota((MAIN, LANES), 0) + MAIN).astype(F32)
    part_ids = iota((parts * wide, LANES), 0) // wide
    tail_keep = iota((wide, MAIN), 0) // 4 == iota((wide, MAIN), 1) // TAIL
    low_half = iota((8, MAIN), 0) < 4

    def step(o, carry):
        total, tails = carry
        block = got[o].astype(F32)
        last = block[wide:]
        tail = jnp.where(low_half, last, pltpu.roll(last, 4, 0))
        tail = jnp.where(tail_keep, jnp.concatenate([tail, tail], axis=0), 0.0)
        values = jnp.concatenate([block[:wide], tail], axis=1)
        codes = jnp.concatenate([last[6:7], last[7:8]], axis=1)
        part = jnp.zeros(codes.shape, jnp.int32)
        lead = codes
        for p in range(1, parts):
            above = codes >= float(MAIN << p)
            part = jnp.where(above, p, part)
            lead = jnp.where(above, codes * (0.5**p), lead)
        spread = jnp.where(part_ids == part, jnp.concatenate([values] * parts, axis=0), 0.0)
        total = total + mxu(one_hot(row_ids == lead), spread.astype(BF16), NT)
        return total, tails + last

    total, tails = lax.fori_loop(
        0,
        owners,
        step,
        (jnp.zeros((MAIN, parts * wide), F32), jnp.zeros((8, MAIN), F32)),
        unroll=8,
    )
    total = total.T
    for p in range(parts):
        cold[:, p * MAIN : (p + 1) * MAIN] = total[p * wide : (p + 1) * wide]
    hot[...] = tails[4:5] + tails[5:6]


def local(
    embedded,
    gate,
    pre_hidden,
    hidden_weight,
    cross_weight,
    out_weight,
    upstream,
    hot_rows,
    cold_owner,
    cold_rows,
    hot_flag,
    bag_sizes,
):
    owners = lax.axis_size("dp")
    groups = lax.axis_size("col")
    samples, cols = embedded.shape
    inner = groups // SIDE
    total_cols = cross_weight.shape[1]
    wide = cols // F
    slots = hot_rows.shape[1]
    side = lax.axis_index("dp") % 2
    group = lax.axis_index("col")
    outer_place = jnp.stack([group // inner, side]).astype(jnp.int32)
    inner_place = jnp.stack([group % inner, side]).astype(jnp.int32)

    outer_rows = total_cols // SIDE

    def shift(x, along_outer, turn):
        pairs = []
        for d in range(owners):
            for g in range(groups):
                outer, rest = divmod(g, inner)
                here = outer if along_outer else rest
                if turn is None:
                    other = (here + 2) % SIDE
                else:
                    other = here ^ 1 if (d + turn) % 2 == 0 else SIDE - 1 - here
                to = other * inner + rest if along_outer else outer * inner + other
                pairs.append((d * groups + g, d * groups + to))
        return lax.ppermute(x, ("dp", "col"), pairs)

    def onward(second, first):
        return (second.astype(F32) + first.astype(F32)).astype(BF16)

    def exchange(blocks, along_outer, work=None, held=(), parts=()):
        diagonal, near, second, own = blocks
        if work is not None:
            held, diagonal = lax.optimization_barrier((held, diagonal))
        first = shift(diagonal, along_outer, 0)
        near = shift(near, along_outer, 0)
        done = ()
        if work is not None:
            done = tuple(work(held))
            first, done = lax.optimization_barrier((first, done))
        far = onward(second, first)
        if not parts:
            return (own, near, shift(far, along_outer, 1)), done, parts
        far, parts = lax.optimization_barrier((far, parts))
        far = shift(far, along_outer, 1)
        w_near, w_far, w_diag = parts
        w_diag = shift(w_diag, True, None)
        near, w_near, w_far = lax.optimization_barrier((near, w_near, w_far))
        parts = w_diag, shift(w_near, True, 0), shift(w_far, True, 1)
        far, parts = lax.optimization_barrier((far, parts))
        return (own, near, far), done, parts

    state = [jax.ShapeDtypeStruct((owners, CAP), F32)] * 3
    state += [jax.ShapeDtypeStruct((owners, MAIN), F32)]
    chunks = cold_owner.shape[0] // 512

    def plan(begin, end, out_shape, scratch=()):
        return lambda held: call(
            functools.partial(plan_kernel, begin, end),
            out_shape,
            held,
            scratch=scratch,
            flops=5 * 10**8,
            moved=0,
        )

    routing = [jax.ShapeDtypeStruct((owners, LANES), F32)] * 3
    slots_in = (cold_owner.T, cold_rows.T, hot_flag.T, bag_sizes[None, :])
    live = lax.broadcasted_iota(jnp.int32, hot_rows.shape, 1) < bag_sizes[:, None]
    hot_index = (
        jnp.where(live & (hot_flag == 1), hot_rows, -1)
        .T.reshape(slots, samples, F)
        .transpose(0, 2, 1)
        .reshape(slots * F, samples)
    )

    def stage_two(terms):
        return call(
            mid_kernel,
            blocks_of(cols, samples) + blocks_of(cols, outer_rows),
            terms + (cross_weight,),
            smem=(inner_place, outer_place),
            scratch=[pltpu.VMEM((outer_rows, samples), BF16)],
            flops=4 * outer_rows * samples,
            moved=10 * outer_rows * samples,
        )

    blocks = call(
        hidden_kernel,
        blocks_of(outer_rows, samples),
        (hidden_weight, pre_hidden, upstream[None, :], out_weight[None, :]),
        smem=(outer_place,),
        flops=2 * total_cols * samples * pre_hidden.shape[1],
        moved=4 * total_cols * samples,
    )
    terms, _, _ = exchange(blocks, True)
    *blocks, w_diag, w_near, w_far, w_own = stage_two(terms)
    terms, planned, parts = exchange(
        blocks, False, plan(0, chunks // 2, state), slots_in, (w_near, w_far, w_diag)
    )
    weights = (w_own, *parts)
    back_one, gated = call(
        gate_kernel,
        [jax.ShapeDtypeStruct((cols, samples), F32), jax.ShapeDtypeStruct((cols, samples), BF16)],
        terms + (embedded,),
        flops=4 * cols * samples,
        moved=16 * cols * samples,
    )
    diagonal = shift(gated, True, None)
    near = shift(gated, True, 0)
    far = shift(gated, True, 1)
    blocks = call(
        cross_kernel,
        blocks_of(cols, samples),
        weights + (gated, diagonal, near, far),
        smem=(inner_place,),
        scratch=[pltpu.VMEM((outer_rows, samples), BF16)],
        flops=2 * total_cols * samples * cols,
        moved=4 * outer_rows * samples,
    )
    terms, routes, _ = exchange(
        blocks, False, plan(chunks // 2, chunks, routing, [pltpu.VMEM(x.shape, F32) for x in state]), slots_in + planned
    )
    message = call(
        send_kernel,
        jax.ShapeDtypeStruct((owners, MSG_ROWS, MAIN), BF16),
        terms + (back_one, gate, *routes, hot_index),
        scratch=[pltpu.VMEM((owners, cols), F32)],
        flops=2 * 10**9,
        moved=10**7,
    )
    got = lax.all_to_all(message, "dp", split_axis=0, concat_axis=0, tiled=True)
    cold_grad, hot_sum = call(
        gather_kernel,
        [
            jax.ShapeDtypeStruct((wide, COLD_DEV), F32),
            jax.ShapeDtypeStruct((1, MAIN), F32),
        ],
        (got,),
        flops=2 * 10**9,
        moved=10**7,
    )
    hot_grad = hot_sum.reshape(HOT // owners, wide).T
    return (hot_grad, cold_grad)


def solution(mesh):
    in_specs = (
        P("dp", "col"),
        P("dp", "col"),
        P("dp", "col"),
        P(None, "col"),
        P("col", None),
        P("col"),
        P("dp"),
        P("dp", None),
        P("dp", None),
        P("dp", None),
        P("dp", None),
        P("dp"),
    )
    out_specs = (P("col", "dp"), P("col", "dp"))
    return jax.shard_map(local, mesh=mesh, in_specs=in_specs, out_specs=out_specs, check_vma=False)
```
